128 devices in a mesh: uly: 8 (over y, z_hi), blk: 16 (over z_lo, x, core).
Axes of the slice: x: 4, y: 4, z: 4 (z_hi: 2, z_lo: 2; z = z_hi * 2 + z_lo), core: 2. Of those that a mesh axis runs over, the one named last changes fastest.
Arguments:
- query_rows: bfloat16 [16384, 1024], P(('uly', 'blk')), may hold values from -160 to 160, as said below
- key_rows: bfloat16 [16384, 1024], P(('uly', 'blk')), may hold values from -6 to 6, as said below
- value_rows: bfloat16 [16384, 1024], P(('uly', 'blk')), may hold values from -6 to 6
- tangent_query: bfloat16 [16384, 1024], P(('uly', 'blk')), may hold values from -6 to 6
- tangent_key: bfloat16 [16384, 1024], P(('uly', 'blk')), may hold values from -6 to 6
- tangent_value: bfloat16 [16384, 1024], P(('uly', 'blk')), may hold values from -6 to 6
Outputs:
- attended: bfloat16 [16384, 1024], P(('uly', 'blk'))
- tangent_out: bfloat16 [16384, 1024], P(('uly', 'blk'))
The draws below stay inside these ranges and needn't reach their ends.
Inputs may be any that keep to these rules, and one draw needn't show every extreme that they name: `query_rows`: queries of order one in most rows. `key_rows`: keys of order one.
All inputs are finite; a program needn't handle non-finite values.
Results may differ from the reference program's by a relative error of at most 0.009.
Values may be sent and summed in bfloat16 or wider, within the bound.
No kernel may reach another device: no remote copies, remote signals or barrier semaphores. Data moves between devices by JAX's collectives and lax.ppermute only.
A program may use at most 128 MiB of HBM per device.

```python
import math
import jax
import jax.numpy as jnp
from jax import lax

HD = 128
HEADS = 8
COLUMNS = 1024
SEQ = 16384


def common_keys(key):
    stride = SEQ // 32
    base = jnp.clip(jax.random.normal(jax.random.fold_in(key, 5), (SEQ, COLUMNS), jnp.float32), -5.0, 5.0)
    noise = jax.random.normal(jax.random.fold_in(key, 6), (SEQ // stride, COLUMNS), jnp.float32)
    return base.at[1::stride].set(base[0::stride] + 0.1 * noise)


def draw_key_rows(key, part):
    return common_keys(key).astype(jnp.bfloat16)


def draw_query_rows(key, part):
    key = jax.random.fold_in(key, 11)
    base = jnp.clip(2.5 * jax.random.normal(jax.random.fold_in(key, 1), (SEQ, COLUMNS), jnp.float32), -12.5, 12.5)
    return base.astype(jnp.bfloat16)


def block_levels(key, shape, shards, low, largest):
    gain, own = 1.0, jax.random.fold_in(key, 6)
    for axis_at, shards_of in shards:
        draws = jnp.exp(jax.random.uniform(jax.random.fold_in(own, axis_at), (shards_of,), jnp.float32, low / len(shards), largest / len(shards)))
        gain = gain * jnp.repeat(draws, shape[axis_at] // shards_of).reshape([-1 if axis == axis_at else 1 for axis in range(len(shape))])
    return gain


def gaussian(rng, shape, deviation, bound, cuts=(), held_as=jnp.bfloat16):
    values = deviation * jax.random.normal(rng, shape, jnp.float32)
    if cuts:
        values = values * block_levels(rng, shape, cuts, -0.22, 0.18)
    return jnp.clip(values, -bound, bound).astype(held_as)


def setup_inputs(seed: int = 0) -> dict:
    keys = jax.random.split(jax.random.key(seed), 7)
    return {
        "query_rows": draw_query_rows(jax.random.fold_in(keys[6], 71), 0),
        "key_rows": draw_key_rows(jax.random.fold_in(keys[6], 71), 0),
        "value_rows": gaussian(keys[2], (SEQ, COLUMNS), 1.0, 6.0, ((0, 128),)),
        "tangent_query": gaussian(keys[3], (SEQ, COLUMNS), 1.0, 6.0, ((0, 128),)),
        "tangent_key": gaussian(keys[4], (SEQ, COLUMNS), 1.0, 6.0, ((0, 128),)),
        "tangent_value": gaussian(keys[5], (SEQ, COLUMNS), 1.0, 6.0, ((0, 128),)),
    }


def head_block(query_block, tquery_block, key_head, value_head, tkey_head, tvalue_head):
    factor = 1.0 / math.sqrt(HD)
    scores = factor * jnp.dot(query_block, key_head.T, preferred_element_type=jnp.float32)
    tangent_scores = factor * (jnp.dot(tquery_block, key_head.T, preferred_element_type=jnp.float32) + jnp.dot(query_block, tkey_head.T, preferred_element_type=jnp.float32))
    peak = lax.optimization_barrier(jnp.max(scores, axis=1, keepdims=True))
    weights = jnp.exp(scores - peak)
    total = lax.optimization_barrier(jnp.sum(weights, axis=1, keepdims=True))
    product = weights * tangent_scores
    tilt = lax.optimization_barrier(jnp.sum(product, axis=1, keepdims=True))
    weights_low = weights.astype(jnp.bfloat16)
    tangent_weights = product.astype(jnp.bfloat16)
    mixed = jnp.dot(weights_low, value_head, preferred_element_type=jnp.float32)
    tangent_mixed = jnp.dot(tangent_weights, value_head, preferred_element_type=jnp.float32) + jnp.dot(weights_low, tvalue_head, preferred_element_type=jnp.float32)
    attended = (mixed / total).astype(jnp.bfloat16)
    tangent_out = ((tangent_mixed - tilt / total * mixed) / total).astype(jnp.bfloat16)
    return (attended, tangent_out)

def split_heads(array):
    return array.reshape(SEQ, HEADS, HD).transpose(1, 0, 2)

def reference(query_rows, key_rows, value_rows, tangent_query, tangent_key, tangent_value):
    rows_block = min(SEQ, 1024)
    count = SEQ // rows_block
    heads_all = (split_heads(query_rows), split_heads(tangent_query), split_heads(key_rows), split_heads(value_rows), split_heads(tangent_key), split_heads(tangent_value))

    def one_head(pieces):
        query_head, tquery_head, key_head, value_head, tkey_head, tvalue_head = pieces

        def one_block(blocks):
            return head_block(blocks[0], blocks[1], key_head, value_head, tkey_head, tvalue_head)
        outs_a, outs_b = lax.map(one_block, (query_head.reshape(count, rows_block, HD), tquery_head.reshape(count, rows_block, HD)))
        return (outs_a.reshape(SEQ, HD), outs_b.reshape(SEQ, HD))
    attended, tangent_out = lax.map(one_head, heads_all)
    attended = attended.transpose(1, 0, 2).reshape(SEQ, COLUMNS)
    tangent_out = tangent_out.transpose(1, 0, 2).reshape(SEQ, COLUMNS)
    return (attended, tangent_out)
```

```python
import functools
import math

import jax
import jax.numpy as jnp
from jax import lax
from jax.experimental import pallas as pl
from jax.experimental.pallas import tpu as pltpu
from jax.sharding import PartitionSpec as P

WIDTH = 128
FACTOR = 1.0 / math.sqrt(WIDTH)
TO_LOG2 = FACTOR * math.log2(math.e)
ROWS_GROUP = 512
MIB = 2**20
WHOLE = pl.BlockSpec(memory_space=pltpu.VMEM)


def dot(a, b):
    return jnp.dot(a, b, preferred_element_type=jnp.float32)


def dot_rows(a, b):
    return lax.dot_general(a, b, (((1,), (1,)), ((), ())), preferred_element_type=jnp.float32)


def call(kernel, outs, operands, limit=24, **cost):
    return pl.pallas_call(
        kernel,
        in_specs=[WHOLE] * len(operands),
        out_specs=[WHOLE] * len(outs),
        out_shape=[jax.ShapeDtypeStruct(shape, dtype) for shape, dtype in outs],
        cost_estimate=pl.CostEstimate(
            flops=cost.get("flops", 0),
            transcendentals=cost.get("transcendentals", 0),
            bytes_accessed=cost.get("bytes_accessed", 2 * MIB),
        ),
        compiler_params=pltpu.CompilerParams(vmem_limit_bytes=limit * MIB),
    )(*operands)


def pack_kernel(q, k, v, tq, tk, tv, queries, *halves):
    heads = queries.shape[0]
    for h in range(heads):
        columns = slice(h * WIDTH, (h + 1) * WIDTH)
        queries[h, :, :WIDTH] = tq[:, columns]
        queries[h, :, WIDTH:] = q[:, columns]
        for number, half in enumerate(halves):
            size = half.shape[1]
            rows = slice(number * size, (number + 1) * size)
            for place, source in enumerate((k, tk, v, tv)):
                half[h, :, place * WIDTH : (place + 1) * WIDTH] = source[rows, columns]


def join_lanes(peak, total, tilt):
    lane = lax.broadcasted_iota(jnp.int32, peak.shape, 1)
    return jnp.where(lane == 0, peak, jnp.where(lane == 1, total, tilt))


def attend_kernel(count_queries, count_pieces, first, *refs):
    queries = refs[:count_queries]
    pieces = refs[count_queries : count_queries + count_pieces]
    states = refs[count_queries + count_pieces : -count_queries]
    outs = refs[-count_queries:]
    rows = queries[0].shape[0]
    size = min(ROWS_GROUP, rows)
    groups = [(part, start) for part in range(count_queries) for start in range(0, rows, size)]

    def scores_of(part, start):
        q = queries[part][start : start + size, WIDTH:]
        scores = [TO_LOG2 * dot_rows(q, piece[:, :WIDTH]) for piece in pieces]
        tiles = [s[:, c : c + WIDTH] for s in scores for c in range(0, s.shape[1], WIDTH)]
        return scores, functools.reduce(jnp.maximum, tiles)

    def absorb(part, start, scores, lanes_peak):
        span = slice(start, start + size)
        both = queries[part][span, :]
        peak = jnp.max(lanes_peak, axis=1, keepdims=True)
        if not first:
            old = states[part][span, 2 * WIDTH :]
            peak = jnp.maximum(old[:, 0:1], peak)
        wide = jnp.broadcast_to(peak, (size, WIDTH))
        lanes_total = by_weights = by_product = None
        for s, piece in zip(scores, pieces):
            keys = s.shape[1]
            weights = jnp.exp2(s - jnp.concatenate([wide] * (keys // WIDTH), axis=1))
            for c in range(0, keys, WIDTH):
                tile = weights[:, c : c + WIDTH]
                lanes_total = tile if lanes_total is None else lanes_total + tile
            product = weights * dot_rows(both, piece[:, : 2 * WIDTH])
            values = piece[:, 2 * WIDTH :]
            ones = jnp.ones((keys, WIDTH), jnp.bfloat16)
            one = dot(weights.astype(jnp.bfloat16), values)
            two = dot(product.astype(jnp.bfloat16), jnp.concatenate([values[:, :WIDTH], ones], axis=1))
            by_weights = one if by_weights is None else by_weights + one
            by_product = two if by_product is None else by_product + two
        total = jnp.broadcast_to(jnp.sum(lanes_total, axis=1, keepdims=True), (size, WIDTH))
        mixed = by_weights[:, :WIDTH]
        tangent = by_weights[:, WIDTH:] + FACTOR * by_product[:, :WIDTH]
        tilt = FACTOR * by_product[:, WIDTH:]
        if not first:
            rescale = jnp.broadcast_to(jnp.exp2(old[:, 0:1] - peak), (size, WIDTH))
            mixed = mixed + rescale * states[part][span, :WIDTH]
            tangent = tangent + rescale * states[part][span, WIDTH : 2 * WIDTH]
            total = total + rescale * old[:, 1:2]
            tilt = tilt + rescale * old[:, 2:3]
        outs[part][span, :WIDTH] = mixed
        outs[part][span, WIDTH : 2 * WIDTH] = tangent
        outs[part][span, 2 * WIDTH :] = join_lanes(wide, total, tilt)

    current = scores_of(*groups[0])
    for number, group in enumerate(groups):
        following = scores_of(*groups[number + 1]) if number + 1 < len(groups) else None
        absorb(*group, *current)
        current = following


def attend(queries, pieces, states):
    rows = queries[0].shape[0]
    keys = sum(piece.shape[0] for piece in pieces)
    pairs = len(queries) * rows * keys
    return call(
        functools.partial(attend_kernel, len(queries), len(pieces), not states),
        [((rows, 3 * WIDTH), jnp.float32)] * len(queries),
        (*queries, *pieces, *states),
        limit=32,
        flops=pairs * WIDTH * 2 * 8,
        transcendentals=pairs,
        bytes_accessed=keys * 1024 + len(queries) * rows * 3584,
    )


def finish_kernel(mine, other, out):
    a, b = mine[:, 2 * WIDTH :], other[:, 2 * WIDTH :]
    shape = (mine.shape[0], WIDTH)
    peak = jnp.maximum(a[:, 0:1], b[:, 0:1])
    scale_a = jnp.broadcast_to(jnp.exp2(a[:, 0:1] - peak), shape)
    scale_b = jnp.broadcast_to(jnp.exp2(b[:, 0:1] - peak), shape)
    total = scale_a * a[:, 1:2] + scale_b * b[:, 1:2]
    tilt = scale_a * a[:, 2:3] + scale_b * b[:, 2:3]
    mixed = scale_a * mine[:, :WIDTH] + scale_b * other[:, :WIDTH]
    tangent = scale_a * mine[:, WIDTH : 2 * WIDTH] + scale_b * other[:, WIDTH : 2 * WIDTH]
    attended = mixed / total
    result = (tangent - tilt * attended) / total
    out[:, :WIDTH] = attended.astype(jnp.bfloat16)
    out[:, WIDTH:] = result.astype(jnp.bfloat16)


def unpack_kernel(blocks, attended, tangent):
    for h in range(blocks.shape[0]):
        columns = slice(h * WIDTH, (h + 1) * WIDTH)
        attended[:, columns] = blocks[h, :, :WIDTH]
        tangent[:, columns] = blocks[h, :, WIDTH:]


def moved(value, dz=0, dx=0, dcore=0):
    def target(index):
        z, x, core = index // 8, index // 2 % 4, index % 2
        return ((z + dz) % 2 * 4 + (x + dx) % 4) * 2 + (core + dcore) % 2

    return lax.ppermute(value, "blk", [(index, target(index)) for index in range(16)])


def exchange(blocks):
    return lax.all_to_all(blocks, "uly", split_axis=0, concat_axis=0, tiled=True)


def on_device(query_rows, key_rows, value_rows, tangent_query, tangent_key, tangent_value):
    tokens, columns = query_rows.shape
    heads = columns // WIDTH
    low = jnp.bfloat16
    queries, half_a, half_b = call(
        pack_kernel,
        [((heads, tokens, 2 * WIDTH), low)] + [((heads, tokens // 2, 4 * WIDTH), low)] * 2,
        (query_rows, key_rows, value_rows, tangent_query, tangent_key, tangent_value),
    )
    own_a = exchange(half_a).reshape(-1, 4 * WIDTH)
    queries = exchange(queries).reshape(-1, 2 * WIDTH)
    own_b = exchange(half_b).reshape(-1, 4 * WIDTH)
    queries = (queries, moved(queries, dcore=1))

    left_a, right_a, across_a = moved(own_a, dx=1), moved(own_a, dx=-1), moved(own_a, dz=1)
    far_a, across_left_a, across_right_a = moved(right_a, dx=-1), moved(across_a, dx=1), moved(right_a, dz=1)
    across_far_a = moved(across_left_a, dx=1)
    left_b, right_b, across_b = moved(own_b, dx=1), moved(own_b, dx=-1), moved(own_b, dz=1)
    far_b, across_left_b, across_right_b = moved(right_b, dx=-1), moved(across_b, dx=1), moved(right_b, dz=1)
    across_far_b = moved(across_right_b, dx=-1)

    states = ()
    for pieces in (
        (own_a,),
        (left_a, right_a, across_a),
        (own_b, far_a, across_left_a, across_right_a),
        (across_far_a, left_b, right_b, across_b),
        (far_b, across_left_b, across_right_b),
        (across_far_b,),
    ):
        states = attend(queries, pieces, states)
    mine, partner = states
    received = moved(partner, dcore=1)
    (blocks,) = call(finish_kernel, [((tokens * heads, 2 * WIDTH), low)], (mine, received))
    blocks = exchange(blocks.reshape(heads, tokens, 2 * WIDTH))
    return tuple(call(unpack_kernel, [((tokens, columns), low)] * 2, (blocks,)))


def solution(mesh):
    spec = P(("uly", "blk"), None)
    return jax.shard_map(
        on_device,
        mesh=mesh,
        in_specs=(spec,) * 6,
        out_specs=(spec, spec),
        check_vma=False,
    )
```

```python
import functools
import math

import jax
import jax.numpy as jnp
from jax import lax
from jax.experimental import pallas as pl
from jax.experimental.pallas import tpu as pltpu
from jax.sharding import PartitionSpec as P

WIDTH = 128
FACTOR = 1.0 / math.sqrt(WIDTH)
TO_LOG2 = FACTOR * math.log2(math.e)
MIB = 2**20
WHOLE = pl.BlockSpec(memory_space=pltpu.VMEM)


def dot(a, b):
    return jnp.dot(a, b, preferred_element_type=jnp.float32)


def dot_rows(a, b):
    return lax.dot_general(a, b, (((1,), (1,)), ((), ())), preferred_element_type=jnp.float32)


def call(kernel, outs, operands, limit=24, **cost):
    return pl.pallas_call(
        kernel,
        in_specs=[WHOLE] * len(operands),
        out_specs=[WHOLE] * len(outs),
        out_shape=[jax.ShapeDtypeStruct(shape, dtype) for shape, dtype in outs],
        cost_estimate=pl.CostEstimate(
            flops=cost.get("flops", 0),
            transcendentals=cost.get("transcendentals", 0),
            bytes_accessed=cost.get("bytes_accessed", 2 * MIB),
        ),
        compiler_params=pltpu.CompilerParams(vmem_limit_bytes=limit * MIB),
    )(*operands)


def pack_kernel(*refs):
    sources, blocks, scratch, arrived = refs[:6], refs[6], refs[7:13], refs[13]
    copies = [pltpu.make_async_copy(*pair, arrived.at[n]) for n, pair in enumerate(zip(sources, scratch))]
    for copy in copies:
        copy.start()
    for copy in copies:
        copy.wait()
    q, k, v, tq, tk, tv = scratch
    tokens = q.shape[0]
    half = tokens // 2
    for h in range(blocks.shape[0]):
        columns = slice(h * WIDTH, (h + 1) * WIDTH)
        for place, source in enumerate((k, tk, v, tv)):
            blocks[h, :tokens, place * WIDTH : (place + 1) * WIDTH] = source[:, columns]
        for place, source in enumerate((tq, q)):
            blocks[h, tokens:, place * WIDTH : (place + 1) * WIDTH] = source[:half, columns]
            blocks[h, tokens:, (place + 2) * WIDTH : (place + 3) * WIDTH] = source[half:, columns]


def pack(arrays):
    tokens, columns = arrays[0].shape
    shape = (columns // WIDTH, tokens * 3 // 2, 4 * WIDTH)
    return pl.pallas_call(
        pack_kernel,
        in_specs=[pl.BlockSpec(memory_space=pl.ANY)] * 6,
        out_specs=WHOLE,
        out_shape=jax.ShapeDtypeStruct(shape, jnp.bfloat16),
        scratch_shapes=[pltpu.VMEM((tokens, columns), jnp.bfloat16)] * 6 + [pltpu.SemaphoreType.DMA((6,))],
        compiler_params=pltpu.CompilerParams(vmem_limit_bytes=58 * MIB),
    )(*arrays)


def join_lanes(peak, total, tilt):
    lane = lax.broadcasted_iota(jnp.int32, peak.shape, 1)
    return jnp.where(lane == 0, peak, jnp.where(lane == 1, total, tilt))


def attend_kernel(count_queries, count_pieces, first, *refs):
    queries = refs[:count_queries]
    pieces = refs[count_queries : count_queries + count_pieces]
    states = refs[count_queries + count_pieces : -count_queries]
    outs = refs[-count_queries:]
    size = queries[0].shape[0]
    groups = [(part, half) for part in range(count_queries) for half in range(2)]

    def scores_of(part, half):
        q = queries[part][:, (2 * half + 1) * WIDTH : (2 * half + 2) * WIDTH]
        scores = [TO_LOG2 * dot_rows(q, piece[:, :WIDTH]) for piece in pieces]
        tiles = [s[:, c : c + WIDTH] for s in scores for c in range(0, s.shape[1], WIDTH)]
        return scores, functools.reduce(jnp.maximum, tiles)

    def absorb(part, half, scores, lanes_peak):
        span = slice(half * size, (half + 1) * size)
        both = queries[part][:, 2 * half * WIDTH : (2 * half + 2) * WIDTH]
        peak = jnp.max(lanes_peak, axis=1, keepdims=True)
        if not first:
            old = states[part][span, 2 * WIDTH :]
            peak = jnp.maximum(old[:, 0:1], peak)
        wide = jnp.broadcast_to(peak, (size, WIDTH))
        lanes_total = by_weights = by_product = None
        for s, piece in zip(scores, pieces):
            keys = s.shape[1]
            weights = jnp.exp2(s - jnp.concatenate([wide] * (keys // WIDTH), axis=1))
            for c in range(0, keys, WIDTH):
                tile = weights[:, c : c + WIDTH]
                lanes_total = tile if lanes_total is None else lanes_total + tile
            product = weights * dot_rows(both, piece[:, : 2 * WIDTH])
            values = piece[:, 2 * WIDTH :]
            ones = jnp.ones((keys, WIDTH), jnp.bfloat16)
            one = dot(weights.astype(jnp.bfloat16), values)
            two = dot(product.astype(jnp.bfloat16), jnp.concatenate([values[:, :WIDTH], ones], axis=1))
            by_weights = one if by_weights is None else by_weights + one
            by_product = two if by_product is None else by_product + two
        total = jnp.broadcast_to(jnp.sum(lanes_total, axis=1, keepdims=True), (size, WIDTH))
        mixed = by_weights[:, :WIDTH]
        tangent = by_weights[:, WIDTH:] + FACTOR * by_product[:, :WIDTH]
        tilt = FACTOR * by_product[:, WIDTH:]
        if not first:
            rescale = jnp.broadcast_to(jnp.exp2(old[:, 0:1] - peak), (size, WIDTH))
            mixed = mixed + rescale * states[part][span, :WIDTH]
            tangent = tangent + rescale * states[part][span, WIDTH : 2 * WIDTH]
            total = total + rescale * old[:, 1:2]
            tilt = tilt + rescale * old[:, 2:3]
        outs[part][span, :WIDTH] = mixed
        outs[part][span, WIDTH : 2 * WIDTH] = tangent
        outs[part][span, 2 * WIDTH :] = join_lanes(wide, total, tilt)

    current = scores_of(*groups[0])
    for number, group in enumerate(groups):
        following = scores_of(*groups[number + 1]) if number + 1 < len(groups) else None
        absorb(*group, *current)
        current = following


def attend(queries, pieces, states):
    rows = 2 * queries[0].shape[0]
    keys = sum(piece.shape[0] for piece in pieces)
    pairs = len(queries) * rows * keys
    return call(
        functools.partial(attend_kernel, len(queries), len(pieces), not states),
        [((rows, 3 * WIDTH), jnp.float32)] * len(queries),
        (*queries, *pieces, *states),
        limit=32,
        flops=pairs * WIDTH * 2 * 8,
        transcendentals=pairs,
        bytes_accessed=keys * 1024 + len(queries) * rows * 3584,
    )


def finish_kernel(mine, other, out):
    a, b = mine[:, 2 * WIDTH :], other[:, 2 * WIDTH :]
    shape = (mine.shape[0], WIDTH)
    peak = jnp.maximum(a[:, 0:1], b[:, 0:1])
    scale_a = jnp.broadcast_to(jnp.exp2(a[:, 0:1] - peak), shape)
    scale_b = jnp.broadcast_to(jnp.exp2(b[:, 0:1] - peak), shape)
    total = scale_a * a[:, 1:2] + scale_b * b[:, 1:2]
    tilt = scale_a * a[:, 2:3] + scale_b * b[:, 2:3]
    mixed = scale_a * mine[:, :WIDTH] + scale_b * other[:, :WIDTH]
    tangent = scale_a * mine[:, WIDTH : 2 * WIDTH] + scale_b * other[:, WIDTH : 2 * WIDTH]
    attended = mixed / total
    result = (tangent - tilt * attended) / total
    heads, tokens, _ = out.shape
    for number in range(2):
        span = slice(number * shape[0] // 2, (number + 1) * shape[0] // 2)
        place = slice(number * tokens // 2, (number + 1) * tokens // 2)
        for column, value in enumerate((attended, result)):
            part = value[span].astype(jnp.bfloat16).reshape(heads, tokens // 2, WIDTH)
            out[:, place, column * WIDTH : (column + 1) * WIDTH] = part


def unpack_kernel(blocks, attended, tangent):
    for h in range(blocks.shape[0]):
        columns = slice(h * WIDTH, (h + 1) * WIDTH)
        attended[:, columns] = blocks[h, :, :WIDTH]
        tangent[:, columns] = blocks[h, :, WIDTH:]


def moved(value, dz=0, dx=0, dcore=0):
    def target(index):
        z, x, core = index // 8, index // 2 % 4, index % 2
        return ((z + dz) % 2 * 4 + (x + dx) % 4) * 2 + (core + dcore) % 2

    return lax.ppermute(value, "blk", [(index, target(index)) for index in range(16)])


def exchange(blocks):
    return lax.all_to_all(blocks, "uly", split_axis=0, concat_axis=0, tiled=True)


def on_device(query_rows, key_rows, value_rows, tangent_query, tangent_key, tangent_value):
    tokens, columns = query_rows.shape
    heads = columns // WIDTH
    low = jnp.bfloat16
    blocks = pack((query_rows, key_rows, value_rows, tangent_query, tangent_key, tangent_value))
    blocks = exchange(blocks)
    own = blocks[:, :tokens].reshape(-1, 4 * WIDTH)
    own_a, own_b, queries = (part.reshape(-1, 4 * WIDTH) for part in jnp.split(blocks, 3, axis=1))
    queries = (queries, moved(queries, dcore=1))

    left_a, right_a, across = moved(own_a, dx=1), moved(own_a, dx=-1), moved(own, dz=1)
    left_b, right_b = moved(own_b, dx=1), moved(own_b, dx=-1)
    states = attend(queries, (own_a, own_b), ())
    far_a = moved(right_a, dx=-1)
    states = attend(queries, (left_a, right_a), states)
    right_b, across, states = lax.optimization_barrier((right_b, across, states))
    far_b, across_left = moved(right_b, dx=-1), moved(across, dx=1)
    across_right_a, across_right_b = moved(right_a, dz=1), moved(right_b, dz=1)
    states = attend(queries, (left_b, right_b, across), states)
    across_far_a, across_far_b = moved(across_right_a, dx=-1), moved(far_b, dz=1)
    states = attend(queries, (far_a, far_b, across_right_a), states)
    states = attend(queries, (across_left, across_right_b), states)
    states = attend(queries, (across_far_a, across_far_b), states)
    mine, partner = states
    received = moved(partner, dcore=1)
    (blocks,) = call(finish_kernel, [((heads, tokens, 2 * WIDTH), low)], (mine, received))
    blocks = exchange(blocks)
    return tuple(call(unpack_kernel, [((tokens, columns), low)] * 2, (blocks,)))


def solution(mesh):
    spec = P(("uly", "blk"), None)
    return jax.shard_map(
        on_device,
        mesh=mesh,
        in_specs=(spec,) * 6,
        out_specs=(spec, spec),
        check_vma=False,
    )
```

```python
import functools
import math

import jax
import jax.numpy as jnp
from jax import lax
from jax.experimental import pallas as pl
from jax.experimental.pallas import tpu as pltpu
from jax.sharding import PartitionSpec as P

WIDTH = 128
FACTOR = 1.0 / math.sqrt(WIDTH)
TO_LOG2 = FACTOR * math.log2(math.e)
MIB = 2**20
WHOLE = pl.BlockSpec(memory_space=pltpu.VMEM)


def dot(a, b):
    return jnp.dot(a, b, preferred_element_type=jnp.float32)


def dot_rows(a, b):
    return lax.dot_general(a, b, (((1,), (1,)), ((), ())), preferred_element_type=jnp.float32)


def call(kernel, outs, operands, limit=24, **cost):
    return pl.pallas_call(
        kernel,
        in_specs=[WHOLE] * len(operands),
        out_specs=[WHOLE] * len(outs),
        out_shape=[jax.ShapeDtypeStruct(shape, dtype) for shape, dtype in outs],
        cost_estimate=pl.CostEstimate(
            flops=cost.get("flops", 0),
            transcendentals=cost.get("transcendentals", 0),
            bytes_accessed=cost.get("bytes_accessed", 2 * MIB),
        ),
        compiler_params=pltpu.CompilerParams(vmem_limit_bytes=limit * MIB),
    )(*operands)


def pack_kernel(*refs):
    sources, blocks, scratch, arrived = refs[:6], refs[6], refs[7:13], refs[13]
    copies = [pltpu.make_async_copy(*pair, arrived.at[n]) for n, pair in enumerate(zip(sources, scratch))]
    for copy in copies:
        copy.start()
    for copy in copies:
        copy.wait()
    q, k, v, tq, tk, tv = scratch
    tokens = q.shape[0]
    half = tokens // 2
    for h in range(blocks.shape[0]):
        columns = slice(h * WIDTH, (h + 1) * WIDTH)
        for place, source in enumerate((k, tk, v, tv)):
            blocks[h, :tokens, place * WIDTH : (place + 1) * WIDTH] = source[:, columns]
        for place, source in enumerate((tq, q)):
            blocks[h, tokens:, place * WIDTH : (place + 1) * WIDTH] = source[:half, columns]
            blocks[h, tokens:, (place + 2) * WIDTH : (place + 3) * WIDTH] = source[half:, columns]


def pack(arrays):
    tokens, columns = arrays[0].shape
    shape = (columns // WIDTH, tokens * 3 // 2, 4 * WIDTH)
    return pl.pallas_call(
        pack_kernel,
        in_specs=[pl.BlockSpec(memory_space=pl.ANY)] * 6,
        out_specs=WHOLE,
        out_shape=jax.ShapeDtypeStruct(shape, jnp.bfloat16),
        scratch_shapes=[pltpu.VMEM((tokens, columns), jnp.bfloat16)] * 6 + [pltpu.SemaphoreType.DMA((6,))],
        compiler_params=pltpu.CompilerParams(vmem_limit_bytes=58 * MIB),
    )(*arrays)


def join_lanes(peak, total, tilt):
    lane = lax.broadcasted_iota(jnp.int32, peak.shape, 1)
    return jnp.where(lane == 0, peak, jnp.where(lane == 1, total, tilt))


def attend_kernel(count_queries, count_pieces, first, *refs):
    queries = refs[:count_queries]
    pieces = refs[count_queries : count_queries + count_pieces]
    states = refs[count_queries + count_pieces : -count_queries]
    outs = refs[-count_queries:]
    size = queries[0].shape[0]
    groups = [(part, half) for part in range(count_queries) for half in range(2)]

    def scores_of(part, half):
        q = queries[part][:, (2 * half + 1) * WIDTH : (2 * half + 2) * WIDTH]
        scores = [TO_LOG2 * dot_rows(q, piece[:, :WIDTH]) for piece in pieces]
        tiles = [s[:, c : c + WIDTH] for s in scores for c in range(0, s.shape[1], WIDTH)]
        return scores, functools.reduce(jnp.maximum, tiles)

    def absorb(part, half, scores, lanes_peak):
        span = slice(half * size, (half + 1) * size)
        both = queries[part][:, 2 * half * WIDTH : (2 * half + 2) * WIDTH]
        peak = jnp.max(lanes_peak, axis=1, keepdims=True)
        if not first:
            old = states[part][span, 2 * WIDTH :]
            peak = jnp.maximum(old[:, 0:1], peak)
        wide = jnp.broadcast_to(peak, (size, WIDTH))
        lanes_total = by_weights = by_product = None
        for s, piece in zip(scores, pieces):
            keys = s.shape[1]
            weights = jnp.exp2(s - jnp.concatenate([wide] * (keys // WIDTH), axis=1))
            for c in range(0, keys, WIDTH):
                tile = weights[:, c : c + WIDTH]
                lanes_total = tile if lanes_total is None else lanes_total + tile
            product = weights * dot_rows(both, piece[:, : 2 * WIDTH])
            values = piece[:, 2 * WIDTH :]
            ones = jnp.ones((keys, WIDTH), jnp.bfloat16)
            one = dot(weights.astype(jnp.bfloat16), values)
            two = dot(product.astype(jnp.bfloat16), jnp.concatenate([values[:, :WIDTH], ones], axis=1))
            by_weights = one if by_weights is None else by_weights + one
            by_product = two if by_product is None else by_product + two
        total = jnp.broadcast_to(jnp.sum(lanes_total, axis=1, keepdims=True), (size, WIDTH))
        mixed = by_weights[:, :WIDTH]
        tangent = by_weights[:, WIDTH:] + FACTOR * by_product[:, :WIDTH]
        tilt = FACTOR * by_product[:, WIDTH:]
        if not first:
            rescale = jnp.broadcast_to(jnp.exp2(old[:, 0:1] - peak), (size, WIDTH))
            mixed = mixed + rescale * states[part][span, :WIDTH]
            tangent = tangent + rescale * states[part][span, WIDTH : 2 * WIDTH]
            total = total + rescale * old[:, 1:2]
            tilt = tilt + rescale * old[:, 2:3]
        outs[part][span, :WIDTH] = mixed
        outs[part][span, WIDTH : 2 * WIDTH] = tangent
        outs[part][span, 2 * WIDTH :] = join_lanes(wide, total, tilt)

    current = scores_of(*groups[0])
    for number, group in enumerate(groups):
        following = scores_of(*groups[number + 1]) if number + 1 < len(groups) else None
        absorb(*group, *current)
        current = following


def attend(queries, pieces, states):
    rows = 2 * queries[0].shape[0]
    keys = sum(piece.shape[0] for piece in pieces)
    pairs = len(queries) * rows * keys
    return call(
        functools.partial(attend_kernel, len(queries), len(pieces), not states),
        [((rows, 3 * WIDTH), jnp.float32)] * len(queries),
        (*queries, *pieces, *states),
        limit=32,
        flops=pairs * WIDTH * 2 * 8,
        transcendentals=pairs,
        bytes_accessed=keys * 1024 + len(queries) * rows * 3584,
    )


def finish_kernel(mine, other, out):
    a, b = mine[:, 2 * WIDTH :], other[:, 2 * WIDTH :]
    shape = (mine.shape[0], WIDTH)
    peak = jnp.maximum(a[:, 0:1], b[:, 0:1])
    scale_a = jnp.broadcast_to(jnp.exp2(a[:, 0:1] - peak), shape)
    scale_b = jnp.broadcast_to(jnp.exp2(b[:, 0:1] - peak), shape)
    total = scale_a * a[:, 1:2] + scale_b * b[:, 1:2]
    tilt = scale_a * a[:, 2:3] + scale_b * b[:, 2:3]
    mixed = scale_a * mine[:, :WIDTH] + scale_b * other[:, :WIDTH]
    tangent = scale_a * mine[:, WIDTH : 2 * WIDTH] + scale_b * other[:, WIDTH : 2 * WIDTH]
    attended = mixed / total
    result = (tangent - tilt * attended) / total
    heads, tokens, _ = out.shape
    for number in range(2):
        span = slice(number * shape[0] // 2, (number + 1) * shape[0] // 2)
        place = slice(number * tokens // 2, (number + 1) * tokens // 2)
        for column, value in enumerate((attended, result)):
            part = value[span].astype(jnp.bfloat16).reshape(heads, tokens // 2, WIDTH)
            out[:, place, column * WIDTH : (column + 1) * WIDTH] = part


def unpack_kernel(blocks, attended, tangent):
    for h in range(blocks.shape[0]):
        columns = slice(h * WIDTH, (h + 1) * WIDTH)
        attended[:, columns] = blocks[h, :, :WIDTH]
        tangent[:, columns] = blocks[h, :, WIDTH:]


def moved(value, dz=0, dx=0, dcore=0):
    def target(index):
        z, x, core = index // 8, index // 2 % 4, index % 2
        return ((z + dz) % 2 * 4 + (x + dx) % 4) * 2 + (core + dcore) % 2

    return lax.ppermute(value, "blk", [(index, target(index)) for index in range(16)])


def exchange(blocks):
    return lax.all_to_all(blocks, "uly", split_axis=0, concat_axis=0, tiled=True)


def on_device(query_rows, key_rows, value_rows, tangent_query, tangent_key, tangent_value):
    tokens, columns = query_rows.shape
    heads = columns // WIDTH
    low = jnp.bfloat16
    blocks = pack((query_rows, key_rows, value_rows, tangent_query, tangent_key, tangent_value))
    blocks = exchange(blocks)
    own = blocks[:, :tokens].reshape(-1, 4 * WIDTH)
    own_a, own_b, queries = (part.reshape(-1, 4 * WIDTH) for part in jnp.split(blocks, 3, axis=1))
    queries = (queries, moved(queries, dcore=1))

    left_a, right_a, across = moved(own_a, dx=1), moved(own_a, dx=-1), moved(own, dz=1)
    left_b, right_b = moved(own_b, dx=1), moved(own_b, dx=-1)
    states = attend(queries, (own_a, own_b), ())
    far_a = moved(right_a, dx=-1)
    states = attend(queries, (left_a, right_a), states)
    right_b, across, states = lax.optimization_barrier((right_b, across, states))
    far_b, across_left = moved(right_b, dx=-1), moved(across, dx=1)
    across_right_a, across_right_b = moved(right_a, dz=1), moved(right_b, dz=1)
    states = attend(queries, (left_b, right_b, across), states)
    across_far_a, across_far_b = moved(across_right_a, dx=-1), moved(far_b, dz=1)
    states = attend(queries, (far_a, across_right_a), states)
    states = attend(queries, (far_b, across_left, across_right_b), states)
    last = (across_far_a, across_far_b)
    received = moved(*attend(queries[1:], last, states[1:]), dcore=1)
    (mine,) = attend(queries[:1], last, states[:1])
    (blocks,) = call(finish_kernel, [((heads, tokens, 2 * WIDTH), low)], (mine, received))
    blocks = exchange(blocks)
    return tuple(call(unpack_kernel, [((tokens, columns), low)] * 2, (blocks,)))


def solution(mesh):
    spec = P(("uly", "blk"), None)
    return jax.shard_map(
        on_device,
        mesh=mesh,
        in_specs=(spec,) * 6,
        out_specs=(spec, spec),
        check_vma=False,
    )
```

```python
import functools
import math

import jax
import jax.numpy as jnp
from jax import lax
from jax.experimental import pallas as pl
from jax.experimental.pallas import tpu as pltpu
from jax.sharding import PartitionSpec as P

WIDTH = 128
FACTOR = 1.0 / math.sqrt(WIDTH)
TO_LOG2 = FACTOR * math.log2(math.e)
MIB = 2**20
WHOLE = pl.BlockSpec(memory_space=pltpu.VMEM)


def dot(a, b):
    return jnp.dot(a, b, preferred_element_type=jnp.float32)


def dot_rows(a, b):
    return lax.dot_general(a, b, (((1,), (1,)), ((), ())), preferred_element_type=jnp.float32)


def call(kernel, outs, operands, limit=24, **cost):
    return pl.pallas_call(
        kernel,
        in_specs=[WHOLE] * len(operands),
        out_specs=[WHOLE] * len(outs),
        out_shape=[jax.ShapeDtypeStruct(shape, dtype) for shape, dtype in outs],
        cost_estimate=pl.CostEstimate(
            flops=cost.get("flops", 0),
            transcendentals=cost.get("transcendentals", 0),
            bytes_accessed=cost.get("bytes_accessed", 2 * MIB),
        ),
        compiler_params=pltpu.CompilerParams(vmem_limit_bytes=limit * MIB),
    )(*operands)


def pack_kernel(*refs):
    sources, blocks, scratch, arrived = refs[:6], refs[6], refs[7:13], refs[13]
    copies = [pltpu.make_async_copy(*pair, arrived.at[n]) for n, pair in enumerate(zip(sources, scratch))]
    for copy in copies:
        copy.start()
    for copy in copies:
        copy.wait()
    q, k, v, tq, tk, tv = scratch
    tokens = q.shape[0]
    half = tokens // 2
    for h in range(blocks.shape[0]):
        columns = slice(h * WIDTH, (h + 1) * WIDTH)
        for place, source in enumerate((k, tk, v, tv)):
            blocks[h, :tokens, place * WIDTH : (place + 1) * WIDTH] = source[:, columns]
        for place, source in enumerate((tq, q)):
            blocks[h, tokens:, place * WIDTH : (place + 1) * WIDTH] = source[:half, columns]
            blocks[h, tokens:, (place + 2) * WIDTH : (place + 3) * WIDTH] = source[half:, columns]


def pack(arrays):
    tokens, columns = arrays[0].shape
    shape = (columns // WIDTH, tokens * 3 // 2, 4 * WIDTH)
    return pl.pallas_call(
        pack_kernel,
        in_specs=[pl.BlockSpec(memory_space=pl.ANY)] * 6,
        out_specs=WHOLE,
        out_shape=jax.ShapeDtypeStruct(shape, jnp.bfloat16),
        scratch_shapes=[pltpu.VMEM((tokens, columns), jnp.bfloat16)] * 6 + [pltpu.SemaphoreType.DMA((6,))],
        compiler_params=pltpu.CompilerParams(vmem_limit_bytes=58 * MIB),
    )(*arrays)


def join_lanes(peak, total, tilt):
    lane = lax.broadcasted_iota(jnp.int32, peak.shape, 1)
    return jnp.where(lane == 0, peak, jnp.where(lane == 1, total, tilt))


def attend_kernel(count_queries, count_pieces, first, *refs):
    queries = refs[:count_queries]
    pieces = refs[count_queries : count_queries + count_pieces]
    states = refs[count_queries + count_pieces : -count_queries]
    outs = refs[-count_queries:]
    size = queries[0].shape[0]
    groups = [(part, half) for part in range(count_queries) for half in range(2)]

    def scores_of(part, half):
        q = queries[part][:, (2 * half + 1) * WIDTH : (2 * half + 2) * WIDTH]
        scores = [TO_LOG2 * dot_rows(q, piece[:, :WIDTH]) for piece in pieces]
        tiles = [s[:, c : c + WIDTH] for s in scores for c in range(0, s.shape[1], WIDTH)]
        return scores, functools.reduce(jnp.maximum, tiles)

    def absorb(part, half, scores, lanes_peak):
        span = slice(half * size, (half + 1) * size)
        both = queries[part][:, 2 * half * WIDTH : (2 * half + 2) * WIDTH]
        peak = jnp.max(lanes_peak, axis=1, keepdims=True)
        if not first:
            old = states[part][span, 2 * WIDTH :]
            peak = jnp.maximum(old[:, 0:1], peak)
        wide = jnp.broadcast_to(peak, (size, WIDTH))
        lanes_total = by_weights = by_product = None
        for s, piece in zip(scores, pieces):
            keys = s.shape[1]
            weights = jnp.exp2(s - jnp.concatenate([wide] * (keys // WIDTH), axis=1))
            for c in range(0, keys, WIDTH):
                tile = weights[:, c : c + WIDTH]
                lanes_total = tile if lanes_total is None else lanes_total + tile
            product = weights * dot_rows(both, piece[:, : 2 * WIDTH])
            values = piece[:, 2 * WIDTH :]
            ones = jnp.ones((keys, WIDTH), jnp.bfloat16)
            one = dot(weights.astype(jnp.bfloat16), values)
            two = dot(product.astype(jnp.bfloat16), jnp.concatenate([values[:, :WIDTH], ones], axis=1))
            by_weights = one if by_weights is None else by_weights + one
            by_product = two if by_product is None else by_product + two
        total = jnp.broadcast_to(jnp.sum(lanes_total, axis=1, keepdims=True), (size, WIDTH))
        mixed = by_weights[:, :WIDTH]
        tangent = by_weights[:, WIDTH:] + FACTOR * by_product[:, :WIDTH]
        tilt = FACTOR * by_product[:, WIDTH:]
        if not first:
            rescale = jnp.broadcast_to(jnp.exp2(old[:, 0:1] - peak), (size, WIDTH))
            mixed = mixed + rescale * states[part][span, :WIDTH]
            tangent = tangent + rescale * states[part][span, WIDTH : 2 * WIDTH]
            total = total + rescale * old[:, 1:2]
            tilt = tilt + rescale * old[:, 2:3]
        outs[part][span, :WIDTH] = mixed
        outs[part][span, WIDTH : 2 * WIDTH] = tangent
        outs[part][span, 2 * WIDTH :] = join_lanes(wide, total, tilt)

    current = scores_of(*groups[0])
    for number, group in enumerate(groups):
        following = scores_of(*groups[number + 1]) if number + 1 < len(groups) else None
        absorb(*group, *current)
        current = following


def attend(queries, pieces, states):
    rows = 2 * queries[0].shape[0]
    keys = sum(piece.shape[0] for piece in pieces)
    pairs = len(queries) * rows * keys
    return call(
        functools.partial(attend_kernel, len(queries), len(pieces), not states),
        [((rows, 3 * WIDTH), jnp.float32)] * len(queries),
        (*queries, *pieces, *states),
        limit=32,
        flops=pairs * WIDTH * 2 * 8,
        transcendentals=pairs,
        bytes_accessed=keys * 1024 + len(queries) * rows * 3584,
    )


def finish_kernel(mine, other, out):
    a, b = mine[:, 2 * WIDTH :], other[:, 2 * WIDTH :]
    shape = (mine.shape[0], WIDTH)
    peak = jnp.maximum(a[:, 0:1], b[:, 0:1])
    scale_a = jnp.broadcast_to(jnp.exp2(a[:, 0:1] - peak), shape)
    scale_b = jnp.broadcast_to(jnp.exp2(b[:, 0:1] - peak), shape)
    total = scale_a * a[:, 1:2] + scale_b * b[:, 1:2]
    tilt = scale_a * a[:, 2:3] + scale_b * b[:, 2:3]
    mixed = scale_a * mine[:, :WIDTH] + scale_b * other[:, :WIDTH]
    tangent = scale_a * mine[:, WIDTH : 2 * WIDTH] + scale_b * other[:, WIDTH : 2 * WIDTH]
    attended = mixed / total
    result = (tangent - tilt * attended) / total
    heads, tokens, _ = out.shape
    for number in range(2):
        span = slice(number * shape[0] // 2, (number + 1) * shape[0] // 2)
        place = slice(number * tokens // 2, (number + 1) * tokens // 2)
        for column, value in enumerate((attended, result)):
            part = value[span].astype(jnp.bfloat16).reshape(heads, tokens // 2, WIDTH)
            out[:, place, column * WIDTH : (column + 1) * WIDTH] = part


def unpack_kernel(blocks, attended, tangent):
    for h in range(blocks.shape[0]):
        columns = slice(h * WIDTH, (h + 1) * WIDTH)
        attended[:, columns] = blocks[h, :, :WIDTH]
        tangent[:, columns] = blocks[h, :, WIDTH:]


def moved(value, dz=0, dx=0, dcore=0):
    def target(index):
        z, x, core = index // 8, index // 2 % 4, index % 2
        return ((z + dz) % 2 * 4 + (x + dx) % 4) * 2 + (core + dcore) % 2

    return lax.ppermute(value, "blk", [(index, target(index)) for index in range(16)])


def exchange(blocks):
    return lax.all_to_all(blocks, "uly", split_axis=0, concat_axis=0, tiled=True)


def on_device(query_rows, key_rows, value_rows, tangent_query, tangent_key, tangent_value):
    tokens, columns = query_rows.shape
    heads = columns // WIDTH
    low = jnp.bfloat16
    blocks = pack((query_rows, key_rows, value_rows, tangent_query, tangent_key, tangent_value))
    blocks = exchange(blocks)
    own = blocks[:, :tokens].reshape(-1, 4 * WIDTH)
    own_a, own_b, queries = (part.reshape(-1, 4 * WIDTH) for part in jnp.split(blocks, 3, axis=1))
    queries = (queries, moved(queries, dcore=1))

    left_a, right_a, across = moved(own_a, dx=1), moved(own_a, dx=-1), moved(own, dz=1)
    left_b, right_b = moved(own_b, dx=1), moved(own_b, dx=-1)
    states = attend(queries, (own_a, own_b), ())
    far_a = moved(right_a, dx=-1)
    states = attend(queries, (left_a, right_a), states)
    right_b, states = lax.optimization_barrier((right_b, states))
    far_b, across_left = moved(right_b, dx=-1), moved(across, dx=1)
    across_right_a, across_right_b = moved(right_a, dz=1), moved(right_b, dz=1)
    states = attend(queries, (left_b, right_b, across), states)
    across_far_a, across_far_b = moved(across_right_a, dx=-1), moved(far_b, dz=1)
    states = attend(queries, (far_a, across_right_a), states)
    states = attend(queries, (far_b, across_left, across_right_b), states)
    last = (across_far_a, across_far_b)
    received = moved(*attend(queries[1:], last, states[1:]), dcore=1)
    (mine,) = attend(queries[:1], last, states[:1])
    (blocks,) = call(finish_kernel, [((heads, tokens, 2 * WIDTH), low)], (mine, received))
    blocks = exchange(blocks)
    return tuple(call(unpack_kernel, [((tokens, columns), low)] * 2, (blocks,)))


def solution(mesh):
    spec = P(("uly", "blk"), None)
    return jax.shard_map(
        on_device,
        mesh=mesh,
        in_specs=(spec,) * 6,
        out_specs=(spec, spec),
        check_vma=False,
    )
```
